1024 devices in a mesh: wide: 16 (over y, z_hi), narrow: 64 (over z_lo, x, core).
Axes of the slice: x: 8, y: 8, z: 8 (z_hi: 2, z_lo: 4; z = z_hi * 4 + z_lo), core: 2. Of those that a mesh axis runs over, the one named last changes fastest.
Arguments:
- tokens: bfloat16 [256, 14848], P('narrow', 'wide'), may hold values from -6 to 6
- cotangent: bfloat16 [256, 14848], P('narrow', 'wide'), may hold values from -6 to 6
- codes_up: bfloat16 [14848, 30720], P('wide', 'narrow'), may hold values from -6 to 6
- scales_up: float32 [14848, 320], P('wide', 'narrow'), may hold values from 0.0041033262 to 0.012309978
- codes_down: bfloat16 [30720, 14848], P('narrow', 'wide'), may hold values from -6 to 6
- scales_down: float32 [320, 14848], P('narrow', 'wide'), may hold values from 0.0028527216 to 0.008558165
- up_rows: float32 [14848], P('wide'), may hold values from 12.8 to 384
- up_columns: float32 [30720], P('narrow'), may hold values from 12.8 to 384
- down_rows: float32 [30720], P('narrow'), may hold values from 12.8 to 384
- down_columns: float32 [14848], P('wide'), may hold values from 12.8 to 384
Outputs:
- mlp_out: bfloat16 [256, 14848], P('narrow', 'wide')
- input_grad: bfloat16 [256, 14848], P('narrow', 'wide')
- step_up: bfloat16 [14848, 30720], P('wide', 'narrow')
- step_down: bfloat16 [30720, 14848], P('narrow', 'wide')
The draws below stay inside these ranges and needn't reach their ends.
All inputs are finite; a program needn't handle non-finite values.
Results may differ from the reference program's by a relative error of at most 0.0068.
Values may be sent and summed in bfloat16 or wider, within the bound.
No kernel may reach another device: no remote copies, remote signals or barrier semaphores. Data moves between devices by JAX's collectives and lax.ppermute only.
A program may use at most 32 MiB of HBM per device.

```python
import math
import jax
import jax.numpy as jnp
from jax import lax

D = 14848
FF = 30720
QB = 96
TOKENS = 256


def block_scale(stream_key, shape, split, least, top_value):
    gain = 1.0
    for dim, shards_of in split:
        draws = jax.random.uniform(jax.random.fold_in(jax.random.fold_in(stream_key, 6), dim), (shards_of,), jnp.float32, least / len(split), top_value / len(split))
        gain = gain * jnp.repeat(jnp.exp(draws), shape[dim] // shards_of).reshape((-1,) + (1,) * (len(shape) - 1 - dim))
    return gain


def noise(own_key, shape, deviation, reach, cuts=(), kind=jnp.bfloat16):
    array = jax.random.normal(own_key, shape, jnp.float32) * deviation
    if len(cuts) > 0:
        array = block_scale(own_key, shape, cuts, -0.22, 0.18) * array
    return jnp.clip(array, min=-reach, max=reach).astype(kind)


def setup_inputs(seed: int = 0) -> dict:
    key_of = jax.random.split(jax.random.key(seed), 11)
    return {
        "tokens": noise(key_of[0], (TOKENS, D), 1.0, 6.0, ((0, 64), (1, 16))),
        "cotangent": noise(key_of[1], (TOKENS, D), 1.0, 6.0, ((0, 64), (1, 16))),
        "codes_up": noise(key_of[2], (D, FF), 1.0, 6.0, ((0, 16), (1, 64))),
        "scales_up": jnp.clip(jnp.exp(math.log(0.012309978) - 1.0986122 * jax.random.uniform(key_of[3], (D, FF // QB), jnp.float32) ** block_scale(key_of[3], (D, FF // QB), ((0, 16), (1, 64)), -0.2, 0.2)), 0.0041033262, 0.012309978),
        "codes_down": noise(key_of[4], (FF, D), 1.0, 6.0, ((0, 64), (1, 16))),
        "scales_down": jnp.clip(jnp.exp(math.log(0.008558165) - 1.0986123 * jax.random.uniform(key_of[5], (FF // QB, D), jnp.float32) ** block_scale(key_of[5], (FF // QB, D), ((0, 64), (1, 16)), -0.2, 0.2)), 0.0028527216, 0.008558165),
        "up_rows": jnp.clip(jnp.exp(math.log(384.0) - 3.4011974 * jax.random.uniform(key_of[6], (D,), jnp.float32) ** block_scale(key_of[6], (D,), ((0, 16),), -0.2, 0.2)), 12.8, 384.0),
        "up_columns": jnp.clip(jnp.exp(math.log(384.0) - 3.4011974 * jax.random.uniform(key_of[7], (FF,), jnp.float32) ** block_scale(key_of[7], (FF,), ((0, 64),), -0.2, 0.2)), 12.8, 384.0),
        "down_rows": jnp.clip(jnp.exp(math.log(384.0) - 3.4011974 * jax.random.uniform(key_of[8], (FF,), jnp.float32) ** block_scale(key_of[8], (FF,), ((0, 64),), -0.2, 0.2)), 12.8, 384.0),
        "down_columns": jnp.clip(jnp.exp(math.log(384.0) - 3.4011974 * jax.random.uniform(key_of[9], (D,), jnp.float32) ** block_scale(key_of[9], (D,), ((0, 16),), -0.2, 0.2)), 12.8, 384.0),
    }


decay_rate = 0.9
square_eps = 1e-30

def gelu_value(value):
    return 0.5 * value * (1.0 + lax.erf(value * 0.7071067811865476))

def gelu_slope(value):
    return 0.5 * (1.0 + lax.erf(value * 0.7071067811865476)) + value * jnp.exp(-0.5 * value * value) * 0.3989422804014327

def reference(tokens, cotangent, codes_up, scales_up, codes_down, scales_down, up_rows, up_columns, down_rows, down_columns):
    width = QB * 8
    count = FF // width
    groups = width // QB

    def up_block(index):
        start = (index * width).astype(jnp.int32)
        codes = lax.dynamic_slice_in_dim(codes_up, start, width, 1)
        scales = lax.dynamic_slice_in_dim(scales_up, (index * groups).astype(jnp.int32), groups, 1)
        full = codes.astype(jnp.float32).reshape(D, groups, QB) * scales[:, :, None]
        return full.reshape(D, width).astype(jnp.bfloat16)

    def down_block(index):
        start = (index * width).astype(jnp.int32)
        codes = lax.dynamic_slice_in_dim(codes_down, start, width, 0)
        scales = lax.dynamic_slice_in_dim(scales_down, (index * groups).astype(jnp.int32), groups, 0)
        full = codes.astype(jnp.float32).reshape(groups, QB, D) * scales[:, None, :]
        return full.reshape(width, D).astype(jnp.bfloat16)

    def forward(carry, index):
        out_sum, grad_sum = carry
        w_up = up_block(index)
        w_down = down_block(index)
        pre = jnp.dot(tokens, w_up, preferred_element_type=jnp.float32)
        hidden = gelu_value(pre).astype(jnp.bfloat16)
        out_sum = out_sum + jnp.dot(hidden, w_down, preferred_element_type=jnp.float32)
        d_hidden = jnp.dot(cotangent, w_down.T, preferred_element_type=jnp.float32)
        d_pre = (d_hidden * gelu_slope(pre)).astype(jnp.bfloat16)
        grad_sum = grad_sum + jnp.dot(d_pre, w_up.T, preferred_element_type=jnp.float32)
        return ((out_sum, grad_sum), (hidden, d_pre))
    zeros = jnp.zeros((TOKENS, D), jnp.float32)
    indices = jnp.arange(count, dtype=jnp.int32)
    (out_sum, grad_sum), (hiddens, d_pres) = lax.scan(forward, (zeros, zeros), indices)

    def gradients(hidden, d_pre):
        g_up = jnp.dot(tokens.T, d_pre, preferred_element_type=jnp.float32)
        g_down = jnp.dot(hidden.T, cotangent, preferred_element_type=jnp.float32)
        return (g_up, g_down)

    def moments(carry, pieces):
        rows_up, cols_down = carry
        g_up, g_down = gradients(pieces[0], pieces[1])
        sq_up = g_up * g_up + square_eps
        sq_down = g_down * g_down + square_eps
        return ((rows_up + lax.optimization_barrier(jnp.sum(sq_up, axis=1)), cols_down + lax.optimization_barrier(jnp.sum(sq_down, axis=0))), (lax.optimization_barrier(jnp.sum(sq_up, axis=0)), lax.optimization_barrier(jnp.sum(sq_down, axis=1))))
    vector = jnp.zeros((D,), jnp.float32)
    (rowsq_up, colsq_down), (colsq_up, rowsq_down) = lax.scan(moments, (vector, vector), (hiddens, d_pres))
    colsq_up = colsq_up.reshape(FF)
    rowsq_down = rowsq_down.reshape(FF)
    row_new_up = decay_rate * up_rows + (1.0 - decay_rate) * rowsq_up / FF
    col_new_up = decay_rate * up_columns + (1.0 - decay_rate) * colsq_up / D
    row_new_down = decay_rate * down_rows + (1.0 - decay_rate) * rowsq_down / D
    col_new_down = decay_rate * down_columns + (1.0 - decay_rate) * colsq_down / FF
    factor_up = lax.rsqrt(row_new_up / jnp.mean(row_new_up))
    factor_down = lax.rsqrt(row_new_down / jnp.mean(row_new_down))
    inv_col_up = lax.rsqrt(col_new_up).reshape(count, width)
    inv_col_down = lax.rsqrt(col_new_down)
    rows_down_split = factor_down.reshape(count, width)

    def updates(pieces):
        g_up, g_down = gradients(pieces[0], pieces[1])
        step_up = (g_up * factor_up[:, None] * pieces[2][None, :]).astype(jnp.bfloat16)
        step_down = (g_down * pieces[3][:, None] * inv_col_down[None, :]).astype(jnp.bfloat16)
        return (step_up, step_down)
    ups, downs = lax.map(updates, (hiddens, d_pres, inv_col_up, rows_down_split))
    step_up = jnp.moveaxis(ups, 0, 1).reshape(D, FF)
    step_down = downs.reshape(FF, D)
    return (out_sum.astype(jnp.bfloat16), grad_sum.astype(jnp.bfloat16), step_up, step_down)
```

```python
import jax
import jax.numpy as jnp
from jax import lax
from jax.sharding import PartitionSpec as P

D = 14848
FF = 30720
QB = 96


decay_rate = 0.9
square_eps = 1e-30


def gelu_value(value):
    return 0.5 * value * (1.0 + lax.erf(value * 0.7071067811865476))


def gelu_slope(value):
    return (
        0.5 * (1.0 + lax.erf(value * 0.7071067811865476))
        + value * jnp.exp(-0.5 * value * value) * 0.3989422804014327
    )


def contract_last(left, right):
    return lax.dot_general(
        left, right, (((1,), (1,)), ((), ())), preferred_element_type=jnp.float32
    )


def contract_first(left, right):
    return lax.dot_general(
        left, right, (((0,), (0,)), ((), ())), preferred_element_type=jnp.float32
    )


def on_device(
    tokens,
    cotangent,
    codes_up,
    scales_up,
    codes_down,
    scales_down,
    up_rows,
    up_columns,
    down_rows,
    down_columns,
):
    local_width = codes_up.shape[0]
    local_hidden = codes_up.shape[1]
    groups = local_hidden // QB
    own_tokens = tokens.shape[0]
    wide = lax.axis_size("wide")
    narrow = lax.axis_size("narrow")
    chips = narrow // 2
    pairs = [(i, i ^ 1) for i in range(narrow)]
    same_core = [[2 * i + core for i in range(chips)] for core in range(2)]
    packed = jnp.concatenate([tokens, cotangent], axis=0)
    mine = lax.all_to_all(
        jnp.broadcast_to(packed[None], (chips,) + packed.shape),
        "narrow",
        0,
        0,
        axis_index_groups=same_core,
    )
    other = lax.ppermute(mine, "narrow", pairs)
    w_up = (
        (codes_up.astype(jnp.float32).reshape(local_width, groups, QB) * scales_up[:, :, None])
        .reshape(local_width, local_hidden)
        .astype(jnp.bfloat16)
    )
    w_down = (
        (codes_down.astype(jnp.float32).reshape(groups, QB, local_width) * scales_down[:, None, :])
        .reshape(local_hidden, local_width)
        .astype(jnp.bfloat16)
    )
    both = jnp.concatenate([mine, other], axis=0)
    tok_all = both[:, :own_tokens].reshape(-1, local_width)
    cot_all = both[:, own_tokens:].reshape(-1, local_width)
    pre_part = jnp.dot(tok_all, w_up, preferred_element_type=jnp.float32).astype(jnp.bfloat16)
    slope_part = contract_last(cot_all, w_down).astype(jnp.bfloat16)
    parts = jnp.stack(
        [pre_part.reshape(wide, -1, local_hidden), slope_part.reshape(wide, -1, local_hidden)], axis=1
    )
    sums = jnp.sum(lax.all_to_all(parts, "wide", 0, 0).astype(jnp.float32), axis=0)
    pre, d_hidden = sums[0], sums[1]
    hidden = gelu_value(pre).astype(jnp.bfloat16)
    d_pre = (d_hidden * gelu_slope(pre)).astype(jnp.bfloat16)
    acts = jnp.stack([hidden, d_pre], axis=0)
    acts = lax.all_to_all(jnp.broadcast_to(acts[None], (wide,) + acts.shape), "wide", 0, 0)
    hidden = acts[:, 0].reshape(-1, local_hidden)
    d_pre = acts[:, 1].reshape(-1, local_hidden)

    g_up = contract_first(tok_all, d_pre)
    g_down = contract_first(hidden, cot_all)
    sq_up = g_up * g_up + square_eps
    sq_down = g_down * g_down + square_eps
    over_wide = jnp.concatenate(
        [jnp.sum(sq_up, axis=0), jnp.sum(sq_down, axis=1), jnp.sum(up_rows)[None]]
    )
    over_wide = jnp.pad(over_wide, (0, -over_wide.shape[0] % 1024)).reshape(8, -1)
    over_wide = lax.all_to_all(
        jnp.broadcast_to(over_wide[None], (wide,) + over_wide.shape), "wide", 0, 0
    )
    over_wide = jnp.sum(over_wide, axis=0).reshape(-1)
    colsq_up = over_wide[:local_hidden]
    rowsq_down = over_wide[local_hidden : 2 * local_hidden]
    up_rows_total = over_wide[2 * local_hidden]

    stats = jnp.concatenate(
        [
            jnp.sum(sq_up, axis=1),
            jnp.sum(sq_down, axis=0),
            jnp.sum(colsq_up)[None],
            jnp.sum(rowsq_down)[None],
            jnp.sum(down_rows)[None],
        ]
    )
    stats = stats + lax.ppermute(stats, "narrow", pairs)
    totals = stats[2 * local_width :]
    totals_high = totals.astype(jnp.bfloat16)
    totals_low = (totals - totals_high.astype(jnp.float32)).astype(jnp.bfloat16)
    stats = jnp.concatenate([stats[: 2 * local_width].astype(jnp.bfloat16), totals_high, totals_low])
    spare = -(2 * own_tokens * local_width + stats.shape[0]) % (2 * own_tokens * 128)
    stats = jnp.pad(stats, (0, spare)).reshape(2 * own_tokens, -1)

    out_part = jnp.dot(hidden, w_down, preferred_element_type=jnp.float32)
    grad_part = contract_last(d_pre, w_up)
    mixed = jnp.concatenate(
        [
            out_part.reshape(2 * chips, own_tokens, local_width),
            grad_part.reshape(2 * chips, own_tokens, local_width),
        ],
        axis=1,
    )
    from_pair = lax.ppermute(mixed[chips:].astype(jnp.bfloat16), "narrow", pairs)
    mixed = (mixed[:chips] + from_pair.astype(jnp.float32)).astype(jnp.bfloat16)
    mixed = jnp.concatenate(
        [mixed, jnp.broadcast_to(stats[None], (chips,) + stats.shape)], axis=2
    )
    mixed = lax.all_to_all(mixed, "narrow", 0, 0, axis_index_groups=same_core)
    mixed = jnp.sum(mixed.astype(jnp.float32), axis=0)
    mlp_out = mixed[:own_tokens, :local_width].astype(jnp.bfloat16)
    input_grad = mixed[own_tokens:, :local_width].astype(jnp.bfloat16)
    stats = mixed[:, local_width:].reshape(-1)
    rowsq_up = stats[:local_width]
    colsq_down = stats[local_width : 2 * local_width]
    totals = stats[2 * local_width : 2 * local_width + 3] + stats[2 * local_width + 3 : 2 * local_width + 6]

    row_new_up = decay_rate * up_rows + (1.0 - decay_rate) * rowsq_up / FF
    col_new_up = decay_rate * up_columns + (1.0 - decay_rate) * colsq_up / D
    row_new_down = decay_rate * down_rows + (1.0 - decay_rate) * rowsq_down / D
    col_new_down = decay_rate * down_columns + (1.0 - decay_rate) * colsq_down / FF
    mean_up = (decay_rate * up_rows_total + (1.0 - decay_rate) * totals[0] / FF) / D
    mean_down = (decay_rate * totals[2] + (1.0 - decay_rate) * totals[1] / D) / FF
    step_up = (
        g_up * lax.rsqrt(row_new_up / mean_up)[:, None] * lax.rsqrt(col_new_up)[None, :]
    ).astype(jnp.bfloat16)
    step_down = (
        g_down * lax.rsqrt(row_new_down / mean_down)[:, None] * lax.rsqrt(col_new_down)[None, :]
    ).astype(jnp.bfloat16)
    return (mlp_out, input_grad, step_up, step_down)


def solution(mesh):
    return jax.shard_map(
        on_device,
        mesh=mesh,
        in_specs=(
            P("narrow", "wide"),
            P("narrow", "wide"),
            P("wide", "narrow"),
            P("wide", "narrow"),
            P("narrow", "wide"),
            P("narrow", "wide"),
            P("wide"),
            P("narrow"),
            P("narrow"),
            P("wide"),
        ),
        out_specs=(
            P("narrow", "wide"),
            P("narrow", "wide"),
            P("wide", "narrow"),
            P("narrow", "wide"),
        ),
        check_vma=False,
    )
```

```python
import functools

import jax
import jax.numpy as jnp
from jax import lax
from jax.experimental import pallas as pl
from jax.experimental.pallas import tpu as pltpu
from jax.sharding import PartitionSpec as P

D = 14848
FF = 30720
QB = 96

decay_rate = 0.9
square_eps = 1e-30

bf16 = jnp.bfloat16
f32 = jnp.float32

WIDTH = 1024
UNITS = 512
GRAM = 256
SLOPE = UNITS + GRAM
LANES = SLOPE + UNITS
DIGITS = 6
DIGIT_UNIT = 8.0
STATS = 256
SPARE = 160


def gelu_value(value):
    return 0.5 * value * (1.0 + lax.erf(value * 0.7071067811865476))


def gelu_slope(value):
    return (
        0.5 * (1.0 + lax.erf(value * 0.7071067811865476))
        + value * jnp.exp(-0.5 * value * value) * 0.3989422804014327
    )


def mxu(left, right, left_dim=1, right_dim=0):
    return lax.dot_general(
        left, right, (((left_dim,), (right_dim,)), ((), ())), preferred_element_type=f32
    )


def iota(shape, dim):
    return lax.broadcasted_iota(jnp.int32, shape, dim)


def whole_call(kernel, outs, name):
    spec = pl.BlockSpec(memory_space=pltpu.VMEM)
    return lambda *args: pl.pallas_call(
        kernel,
        out_shape=[jax.ShapeDtypeStruct(shape, dtype) for shape, dtype in outs],
        in_specs=[spec] * len(args),
        out_specs=[spec] * len(outs),
        compiler_params=pltpu.CompilerParams(vmem_limit_bytes=24 * 1024 * 1024),
        name=name,
    )(*args)


def weights_kernel(codes_up, scales_up, codes_down, scales_down, w_up, w_down):
    width, units = codes_up.shape
    w_up[...] = jnp.zeros_like(w_up)
    w_down[...] = jnp.zeros_like(w_down)
    lane = iota((width, units), 1)
    scales = scales_up[:, 0:1]
    for group in range(1, units // QB):
        scales = jnp.where(lane >= group * QB, scales_up[:, group : group + 1], scales)
    w_up[:width, :units] = (codes_up[...].astype(f32) * scales).astype(bf16)
    for group in range(units // QB):
        rows = slice(group * QB, (group + 1) * QB)
        w_down[rows, :width] = (
            codes_down[rows, :].astype(f32) * scales_down[group : group + 1, :]
        ).astype(bf16)


def apart(count, own):
    half = count // 2
    row, column = iota((count, count), 0), iota((count, count), 1)
    second = (row >= half).astype(jnp.int32)
    token = row - second * half
    source = (token // own) * (2 * own) + second * own + token % own
    return (column == source).astype(f32).astype(bf16)


def partial_kernel(own, mine, other, w_up, w_down, up_rows, tok, cot, parts):
    count, width = mine.shape
    half = count // 2
    split = apart(count, own)
    for place, ref in ((0, mine), (half, other)):
        rows = mxu(split, ref[...]).astype(bf16)
        tok[place : place + half, :width] = rows[:half]
        cot[place : place + half, :width] = rows[half:]
    tok[:, width:] = jnp.zeros((count, WIDTH - width), bf16)
    cot[:, width:] = jnp.zeros((count, WIDTH - width), bf16)
    tokens, cotangents = tok[...], cot[...]
    parts[:, :UNITS] = mxu(tokens, w_up[...]).astype(bf16)
    row, column = iota((count, count), 0), iota((count, count), 1)
    gram_tok = mxu(tokens, tokens, 1, 1)
    gram_cot = mxu(cotangents, cotangents, 1, 1)
    parts[:, UNITS:SLOPE] = jnp.where(row >= column, gram_tok, gram_cot).astype(bf16)
    diagonal = jnp.sum(jnp.where(row == column, gram_cot, 0.0), axis=1, keepdims=True)
    slope = mxu(cotangents, w_down[...], 1, 1)
    units = UNITS - 32
    lane = iota((count, UNITS), 1)
    slope = jnp.where(lane == units, diagonal, slope)
    rest = jnp.floor(jnp.sum(up_rows[...], axis=1, keepdims=True) * DIGIT_UNIT + 0.5)
    for digit in range(DIGITS):
        shorter = jnp.floor(rest * (1.0 / 16.0))
        slope = jnp.where(lane == units + 1 + digit, rest - 16.0 * shorter, slope)
        rest = shorter
    parts[:, SLOPE:] = slope.astype(bf16)


def mix_kernel(local_hidden, acts, tok, cot, w_up, w_down, down_rows, send, keep, stats, squares):
    count = acts.shape[0]
    half = count // 2
    lane = iota((count, UNITS), 1)
    hidden = acts[:, :UNITS]
    d_wide = acts[:, SLOPE:].astype(f32)
    diagonal = 2.0 * d_wide[:, local_hidden : local_hidden + 1]
    d_wide = jnp.where(lane < local_hidden, d_wide, 0.0)
    d_pre = d_wide.astype(bf16)
    out = mxu(hidden, w_down[...])
    keep[:half, :] = out[:half]
    send[:half, :] = out[half:].astype(bf16)
    grad = mxu(d_pre, w_up[...], 1, 1)
    keep[half:, :] = grad[:half]
    send[half:count, :] = grad[half:].astype(bf16)
    row, column = iota((count, count), 0), iota((count, count), 1)
    gram = acts[:, UNITS:SLOPE].astype(f32)
    lower = jnp.where(row > column, 2.0 * gram, jnp.where(row == column, gram, 0.0)).astype(bf16)
    upper = jnp.where(row < column, 2.0 * gram, 0.0).astype(bf16)
    hidden_wide = hidden.astype(f32)
    colsq_up = jnp.sum(d_wide * mxu(lower, d_pre), axis=0, keepdims=True)
    rowsq_down = jnp.sum(
        hidden_wide * (mxu(upper, hidden) + diagonal * hidden_wide), axis=0, keepdims=True
    )
    real = iota((1, UNITS), 1) < local_hidden
    colsq_up = jnp.where(real, jnp.maximum(colsq_up, 0.0) + D * square_eps, 0.0)
    rowsq_down = jnp.where(real, jnp.maximum(rowsq_down, 0.0) + D * square_eps, 0.0)
    squares[0:1, :] = colsq_up
    squares[1:2, :] = rowsq_down
    totals = [
        jnp.sum(colsq_up, axis=1, keepdims=True),
        jnp.sum(rowsq_down, axis=1, keepdims=True),
        jnp.sum(down_rows[...], axis=1, keepdims=True),
    ]
    g_up = mxu(d_pre, tok[...], 0, 0)
    rowsq_up = jnp.sum(g_up * g_up, axis=0, keepdims=True) + local_hidden * square_eps
    g_down = mxu(hidden, cot[...], 0, 0)
    colsq_down = jnp.sum(g_down * g_down, axis=0, keepdims=True) + local_hidden * square_eps
    spare = iota((1, STATS), 1)
    for place, sums in ((0, rowsq_up), (4, colsq_down)):
        for part in range(4):
            piece = sums[:, part * STATS : (part + 1) * STATS]
            if part == 3:
                piece = jnp.where(spare < SPARE, piece, 0.0)
                for index, total in enumerate(totals):
                    piece = jnp.where(spare == SPARE + index, total, piece)
            stats[place + part : place + part + 1, :] = piece
    block = stats[...]
    high = block.astype(bf16).astype(f32)
    send[count:, :] = jnp.zeros((16, WIDTH), bf16)
    send[count:, :STATS] = jnp.concatenate([high, block - high], axis=0).astype(bf16)


def pair_kernel(own, keep, got, stats, mixed):
    count = keep.shape[0]
    sums = (keep[...] + got[:count, :].astype(f32)).astype(bf16)
    mixed[:, :WIDTH] = mxu(apart(count, own), sums, 0, 0).astype(bf16)
    tail = got[count:, :STATS].astype(f32)
    block = stats[...] + (tail[:8] + tail[8:])
    high = block.astype(bf16).astype(f32)
    low = (iota((8, STATS), 0) == 7) & (iota((8, STATS), 1) >= SPARE)
    block = jnp.where(low, block - high, high)
    mixed[:, WIDTH:] = jnp.concatenate([block] * (count // 8), axis=0).astype(bf16)


def as_column(line, length):
    return jnp.transpose(jnp.broadcast_to(line, (8, line.shape[1])))[:length, 0:1]


def step_kernel(
    own,
    mixed,
    acts,
    tok,
    cot,
    squares,
    up_rows,
    up_columns,
    down_rows,
    down_columns,
    mlp_out,
    input_grad,
    step_up,
    step_down,
):
    width, units = step_up.shape
    count = acts.shape[0]
    sums = jnp.sum(mixed[...].astype(f32).reshape(-1, 2 * own, WIDTH + STATS), axis=0)
    mlp_out[...] = sums[:own, :width].astype(bf16)
    input_grad[...] = sums[own:, :width].astype(bf16)
    block = sums[:, WIDTH:]
    rowsq_up = jnp.concatenate([block[i : i + 1] for i in range(4)], axis=1)
    colsq_down = jnp.concatenate([block[i : i + 1] for i in range(4, 8)], axis=1)
    both = block[3:4] + block[7:8]
    spare = iota((1, STATS), 1)
    total_up, total_down, total_rows = (
        jnp.sum(jnp.where(spare == SPARE + i, both, 0.0), axis=1, keepdims=True) for i in range(3)
    )
    digits = acts[0:16, SLOPE:].astype(f32)[0:1]
    lane = iota((1, UNITS), 1)
    weight = jnp.zeros((1, UNITS), f32)
    for digit in range(DIGITS):
        weight = jnp.where(lane == units + 1 + digit, 2.0 * 16.0**digit / DIGIT_UNIT, weight)
    total_state = jnp.sum(digits * weight, axis=1, keepdims=True)
    mean_up = (decay_rate * total_state + (1.0 - decay_rate) * total_up / FF) / D
    mean_down = (decay_rate * total_rows + (1.0 - decay_rate) * total_down / D) / FF
    keep_rate = 1.0 - decay_rate
    row_new_up = decay_rate * up_rows[...] + keep_rate * rowsq_up[:, :width] / FF
    col_new_down = decay_rate * down_columns[...] + keep_rate * colsq_down[:, :width] / FF
    col_new_up = decay_rate * up_columns[...] + keep_rate * squares[0:1, :units] / D
    row_new_down = decay_rate * down_rows[...] + keep_rate * squares[1:2, :units] / D
    row_up = jnp.concatenate(
        [lax.rsqrt(row_new_up / mean_up), jnp.zeros((1, WIDTH - width), f32)], axis=1
    )
    row_down = jnp.concatenate(
        [lax.rsqrt(row_new_down / mean_down), jnp.zeros((1, UNITS - units), f32)], axis=1
    )
    g_up = mxu(tok[...], acts[:, SLOPE:], 0, 0)[:width, :units]
    step_up[...] = (g_up * as_column(row_up, width) * lax.rsqrt(col_new_up)).astype(bf16)
    g_down = mxu(acts[:, :UNITS], cot[...], 0, 0)[:units, :width]
    step_down[...] = (g_down * as_column(row_down, units) * lax.rsqrt(col_new_down)).astype(bf16)


def on_device(
    tokens,
    cotangent,
    codes_up,
    scales_up,
    codes_down,
    scales_down,
    up_rows,
    up_columns,
    down_rows,
    down_columns,
):
    width, units = codes_up.shape
    own = tokens.shape[0]
    wide = lax.axis_size("wide")
    narrow = lax.axis_size("narrow")
    chips = narrow // 2
    line = wide // 2
    count = own * narrow
    core_pairs = [(i, i ^ 1) for i in range(narrow)]
    same_core = [[2 * i + core for i in range(chips)] for core in range(2)]
    half_pairs = [(i, i ^ 1) for i in range(wide)]
    same_half = [[2 * i + half for i in range(line)] for half in range(2)]
    up_rows, down_rows = up_rows[None], down_rows[None]
    up_columns, down_columns = up_columns[None], down_columns[None]

    packed = jnp.concatenate([tokens, cotangent], axis=0)
    mine = lax.all_to_all(
        jnp.broadcast_to(packed[None], (chips,) + packed.shape),
        "narrow",
        0,
        0,
        axis_index_groups=same_core,
    ).reshape(count, width)
    w_up, w_down = whole_call(
        weights_kernel, [((WIDTH, UNITS), bf16), ((UNITS, WIDTH), bf16)], "weights"
    )(codes_up, scales_up, codes_down, scales_down)
    mine, w_up, w_down = lax.optimization_barrier((mine, w_up, w_down))
    other = lax.ppermute(mine, "narrow", core_pairs)
    tok, cot, parts = whole_call(
        functools.partial(partial_kernel, own),
        [((count, WIDTH), bf16), ((count, WIDTH), bf16), ((count, LANES), bf16)],
        "partial_sums",
    )(mine, other, w_up, w_down, up_rows)

    parts = lax.all_to_all(
        parts.reshape(line, -1, LANES), "wide", 0, 0, axis_index_groups=same_half
    )
    sums = jnp.sum(parts.astype(f32), axis=0)
    sums = sums + lax.ppermute(sums.astype(bf16), "wide", half_pairs).astype(f32)
    pre = sums[:, :UNITS]
    acts = jnp.concatenate(
        [gelu_value(pre), sums[:, UNITS:SLOPE], sums[:, SLOPE:] * gelu_slope(pre)], axis=1
    ).astype(bf16)
    acts = lax.all_to_all(
        jnp.broadcast_to(acts[None], (line,) + acts.shape),
        "wide",
        0,
        0,
        axis_index_groups=same_half,
    ).reshape(count, LANES)

    send, keep, stats, squares = whole_call(
        functools.partial(mix_kernel, units),
        [
            ((count + 16, WIDTH), bf16),
            ((count, WIDTH), f32),
            ((8, STATS), f32),
            ((2, UNITS), f32),
        ],
        "outputs_and_squares",
    )(acts, tok, cot, w_up, w_down, down_rows)
    got = lax.ppermute(send, "narrow", core_pairs)
    (mixed,) = whole_call(
        functools.partial(pair_kernel, own), [((count, WIDTH + STATS), bf16)], "pair_sum"
    )(keep, got, stats)
    mixed = lax.all_to_all(
        mixed.reshape(chips, -1, WIDTH + STATS), "narrow", 0, 0, axis_index_groups=same_core
    ).reshape(count, WIDTH + STATS)
    return tuple(
        whole_call(
            functools.partial(step_kernel, own),
            [
                ((own, width), bf16),
                ((own, width), bf16),
                ((width, units), bf16),
                ((units, width), bf16),
            ],
            "steps",
        )(mixed, acts, tok, cot, squares, up_rows, up_columns, down_rows, down_columns)
    )


def solution(mesh):
    return jax.shard_map(
        on_device,
        mesh=mesh,
        in_specs=(
            P("narrow", "wide"),
            P("narrow", "wide"),
            P("wide", "narrow"),
            P("wide", "narrow"),
            P("narrow", "wide"),
            P("narrow", "wide"),
            P("wide"),
            P("narrow"),
            P("narrow"),
            P("wide"),
        ),
        out_specs=(
            P("narrow", "wide"),
            P("narrow", "wide"),
            P("wide", "narrow"),
            P("narrow", "wide"),
        ),
        check_vma=False,
    )
```

```python
import functools

import jax
import jax.numpy as jnp
from jax import lax
from jax.experimental import pallas as pl
from jax.experimental.pallas import tpu as pltpu
from jax.sharding import PartitionSpec as P

D = 14848
FF = 30720
QB = 96

decay_rate = 0.9
square_eps = 1e-30

bf16 = jnp.bfloat16
f32 = jnp.float32

WIDTH = 1024
UNITS = 512
GRAM = 256
SLOPE = UNITS + GRAM
LANES = SLOPE + UNITS
DIGITS = 6
DIGIT_UNIT = 8.0
STATS = 256
SPARE = 160
CHUNK = 256


def gelu_value(value):
    return 0.5 * value * (1.0 + lax.erf(value * 0.7071067811865476))


def gelu_slope(value):
    return (
        0.5 * (1.0 + lax.erf(value * 0.7071067811865476))
        + value * jnp.exp(-0.5 * value * value) * 0.3989422804014327
    )


def mxu(left, right, left_dim=1, right_dim=0):
    return lax.dot_general(
        left, right, (((left_dim,), (right_dim,)), ((), ())), preferred_element_type=f32
    )


def iota(shape, dim):
    return lax.broadcasted_iota(jnp.int32, shape, dim)


def whole_call(kernel, outs, name, flops=0, scratch=(), out_spaces=None):
    spec = pl.BlockSpec(memory_space=pltpu.VMEM)
    spaces = out_spaces or [pltpu.VMEM] * len(outs)

    def call(*args):
        moved = sum(a.size * a.dtype.itemsize for a in args)
        return pl.pallas_call(
            kernel,
            out_shape=[jax.ShapeDtypeStruct(shape, dtype) for shape, dtype in outs],
            in_specs=[spec] * len(args),
            out_specs=[pl.BlockSpec(memory_space=space) for space in spaces],
            scratch_shapes=list(scratch),
            compiler_params=pltpu.CompilerParams(vmem_limit_bytes=24 * 1024 * 1024),
            cost_estimate=pl.CostEstimate(flops=flops, bytes_accessed=moved, transcendentals=0),
            name=name,
        )(*args)

    return call


def spread_kernel(packed, copies):
    both = packed[...].astype(f32)
    both = jnp.concatenate([both, both], axis=0).astype(bf16)
    for pair in range(copies.shape[0] // 16):
        copies[16 * pair : 16 * pair + 16, :] = both


def weights_kernel(codes_up, scales_up, codes_down, scales_down, up_rows, w_up, w_down, digits, lines):
    width, units = codes_up.shape
    lane = iota((width, units), 1)
    for codes, scales, ref in ((codes_up, scales_up, w_up), (codes_down, scales_down, w_down)):
        lines[...] = jnp.zeros_like(lines)
        lines[: units // QB, :width] = scales[...]
        columns = jnp.transpose(lines[...])[:width]
        spread = columns[:, 0:1]
        for group in range(1, units // QB):
            spread = jnp.where(lane >= group * QB, columns[:, group : group + 1], spread)
        ref[...] = jnp.zeros_like(ref)
        ref[:width, :units] = (codes[...].astype(f32) * spread).astype(bf16)
    place = iota((8, UNITS), 1)
    line = jnp.zeros((8, UNITS), f32)
    rest = jnp.floor(jnp.sum(up_rows[...], axis=1, keepdims=True) * DIGIT_UNIT + 0.5)
    for digit in range(DIGITS):
        shorter = jnp.floor(rest * (1.0 / 16.0))
        line = jnp.where(place == units + 1 + digit, rest - 16.0 * shorter, line)
        rest = shorter
    digits[...] = line


def apart(count, own):
    half = count // 2
    row, column = iota((count, count), 0), iota((count, count), 1)
    second = (row >= half).astype(jnp.int32)
    token = row - second * half
    source = (token // own) * (2 * own) + second * own + token % own
    return (column == source).astype(f32).astype(bf16)


def first_kernel(own, mine, w_up, w_down, tok, cot, pre, slope):
    count, width = mine.shape
    half = count // 2
    rows = mxu(apart(count, own), mine[...]).astype(bf16)
    for ref, first in ((tok, 0), (cot, half)):
        ref[:, WIDTH - 128 :] = jnp.zeros((half, 128), bf16)
        ref[:, :width] = rows[first : first + half]
    pre[...] = mxu(tok[...], w_up[...]).astype(bf16)
    slope[...] = mxu(cot[...], w_down[...])


def partial_kernel(
    own, units, other, tok_own, cot_own, pre_own, slope_own, w_up, w_down, digits, tok, cot, parts
):
    count, width = other.shape
    half = count // 2
    rows = mxu(apart(count, own), other[...]).astype(bf16)
    for ref, first, owned in ((tok, 0, tok_own), (cot, half, cot_own)):
        ref[:half, :] = owned[...]
        ref[half:, WIDTH - 128 :] = jnp.zeros((half, 128), bf16)
        ref[half:, :width] = rows[first : first + half]
    parts[:half, :UNITS] = pre_own[...]
    parts[half:, :UNITS] = mxu(tok[half:, :], w_up[...]).astype(bf16)
    row, column = iota((count, count), 0), iota((count, count), 1)
    tokens, cotangents = tok[...], cot[...]
    gram_tok = mxu(tokens, tokens, 1, 1)
    gram_cot = mxu(cotangents, cotangents, 1, 1)
    parts[:, UNITS:SLOPE] = jnp.where(row >= column, gram_tok, gram_cot).astype(bf16)
    diagonal = jnp.sum(jnp.where(row == column, gram_cot, 0.0), axis=1, keepdims=True)
    lane = iota((half, UNITS), 1)
    extra = digits[0:1, :]
    slope = jnp.where(lane == units, diagonal[:half], slope_own[...] + extra)
    parts[:half, SLOPE:] = slope.astype(bf16)
    slope = mxu(cot[half:, :], w_down[...])
    slope = jnp.where(lane == units, diagonal[half:], slope + extra)
    parts[half:, SLOPE:] = slope.astype(bf16)


def masked_slope(acts, units):
    count = acts.shape[0]
    lane = iota((count, UNITS), 1)
    return jnp.where(lane < units, acts[:, SLOPE:].astype(f32), 0.0)


def send_kernel(units, acts, tok, cot, w_up, w_down, down_rows, send, stats, squares):
    count = acts.shape[0]
    half = count // 2
    hidden = acts[:, :UNITS]
    d_wide = masked_slope(acts, units)
    diagonal = 2.0 * acts[:, SLOPE:].astype(f32)[:, units : units + 1]
    d_pre = d_wide.astype(bf16)
    send[:half, :] = mxu(hidden[half:], w_down[...], 1, 1).astype(bf16)
    send[half:count, :] = mxu(d_pre[half:], w_up[...], 1, 1).astype(bf16)
    row, column = iota((count, count), 0), iota((count, count), 1)
    gram = acts[:, UNITS:SLOPE].astype(f32)
    lower = jnp.where(row > column, 2.0 * gram, jnp.where(row == column, gram, 0.0)).astype(bf16)
    upper = jnp.where(row < column, 2.0 * gram, 0.0).astype(bf16)
    hidden_wide = hidden.astype(f32)
    colsq_up = jnp.sum(d_wide * mxu(lower, d_pre), axis=0, keepdims=True)
    rowsq_down = jnp.sum(
        hidden_wide * (mxu(upper, hidden) + diagonal * hidden_wide), axis=0, keepdims=True
    )
    real = iota((1, UNITS), 1) < units
    colsq_up = jnp.where(real, jnp.maximum(colsq_up, 0.0) + D * square_eps, 0.0)
    rowsq_down = jnp.where(real, jnp.maximum(rowsq_down, 0.0) + D * square_eps, 0.0)
    squares[0:1, :] = colsq_up
    squares[1:2, :] = rowsq_down
    totals = [
        jnp.sum(colsq_up, axis=1, keepdims=True),
        jnp.sum(rowsq_down, axis=1, keepdims=True),
        jnp.sum(down_rows[...], axis=1, keepdims=True),
    ]
    g_up = mxu(d_pre, tok[...], 0, 0)
    rowsq_up = jnp.sum(g_up * g_up, axis=0, keepdims=True) + units * square_eps
    g_down = mxu(hidden, cot[...], 0, 0)
    colsq_down = jnp.sum(g_down * g_down, axis=0, keepdims=True) + units * square_eps
    spare = iota((1, STATS), 1)
    for place, sums in ((0, rowsq_up), (4, colsq_down)):
        for part in range(4):
            piece = sums[:, part * STATS : (part + 1) * STATS]
            if part == 3:
                piece = jnp.where(spare < SPARE, piece, 0.0)
                for index, total in enumerate(totals):
                    piece = jnp.where(spare == SPARE + index, total, piece)
            stats[place + part : place + part + 1, :] = piece
    block = stats[...]
    high = block.astype(bf16).astype(f32)
    send[count:, :] = jnp.zeros((16, WIDTH), bf16)
    send[count:, :STATS] = jnp.concatenate([high, block - high], axis=0).astype(bf16)


def keep_kernel(units, acts, w_up, w_down, keep):
    half = acts.shape[0] // 2
    keep[:half, :] = mxu(acts[:half, :UNITS], w_down[...], 1, 1)
    d_pre = masked_slope(acts, units)[:half].astype(bf16)
    keep[half:, :] = mxu(d_pre, w_up[...], 1, 1)


def pair_kernel(own, keep, got, stats, mixed):
    count = keep.shape[0]
    sums = (keep[...] + got[:count, :].astype(f32)).astype(bf16)
    mixed[:, :WIDTH] = mxu(apart(count, own), sums, 0, 0).astype(bf16)
    tail = got[count:, :STATS].astype(f32)
    block = stats[...] + (tail[:8] + tail[8:])
    high = block.astype(bf16).astype(f32)
    low = (iota((8, STATS), 0) == 7) & (iota((8, STATS), 1) >= SPARE)
    block = jnp.where(low, block - high, high)
    mixed[:, WIDTH:] = jnp.concatenate([block] * (count // 8), axis=0).astype(bf16)


def padded(line, lanes):
    return jnp.concatenate([line, jnp.ones((1, lanes - line.shape[1]), f32)], axis=1)


def step_kernel(
    own,
    units,
    mixed,
    acts,
    tok,
    cot,
    squares,
    up_rows,
    up_columns,
    down_rows,
    down_columns,
    mlp_out,
    input_grad,
    step_up,
    step_down,
    held,
    sems,
):
    width = up_rows.shape[1]
    sums = jnp.sum(mixed[...].astype(f32).reshape(-1, 2 * own, WIDTH + STATS), axis=0)
    mlp_out[...] = sums[:own, :width].astype(bf16)
    input_grad[...] = sums[own:, :width].astype(bf16)
    block = sums[:, WIDTH:]
    rowsq_up = jnp.concatenate([block[i : i + 1] for i in range(4)], axis=1)
    colsq_down = jnp.concatenate([block[i : i + 1] for i in range(4, 8)], axis=1)
    both = block[3:4] + block[7:8]
    spare = iota((1, STATS), 1)
    total_up, total_down, total_rows = (
        jnp.sum(jnp.where(spare == SPARE + i, both, 0.0), axis=1, keepdims=True) for i in range(3)
    )
    digits = acts[0:16, SLOPE:].astype(f32)[0:1]
    lane = iota((1, UNITS), 1)
    weight = jnp.zeros((1, UNITS), f32)
    for digit in range(DIGITS):
        weight = jnp.where(lane == units + 1 + digit, 2.0 * 16.0**digit / DIGIT_UNIT, weight)
    total_state = jnp.sum(digits * weight, axis=1, keepdims=True)
    mean_up = (decay_rate * total_state + (1.0 - decay_rate) * total_up / FF) / D
    mean_down = (decay_rate * total_rows + (1.0 - decay_rate) * total_down / D) / FF
    keep_rate = 1.0 - decay_rate
    row_new_up = decay_rate * up_rows[...] + keep_rate * rowsq_up[:, :width] / FF
    col_new_down = decay_rate * down_columns[...] + keep_rate * colsq_down[:, :width] / FF
    lines = jnp.concatenate(
        [
            jnp.broadcast_to(padded(lax.rsqrt(row_new_up) * jnp.sqrt(mean_up), WIDTH), (4, WIDTH)),
            jnp.broadcast_to(
                padded(lax.rsqrt(col_new_down) * jnp.sqrt(mean_down), WIDTH), (4, WIDTH)
            ),
        ],
        axis=0,
    )
    columns = jnp.transpose(lines)
    col_new_up = decay_rate * up_columns[...] + keep_rate * squares[0:1, :units] / D
    row_new_down = decay_rate * down_rows[...] + keep_rate * squares[1:2, :units] / D
    ups = (tok, acts[:, SLOPE:], lax.rsqrt(col_new_up), step_up)
    downs = (cot, acts[:, :UNITS], lax.rsqrt(row_new_down), step_down)
    copies = []
    for first in range(0, width, CHUNK):
        rows = slice(first, min(first + CHUNK, width))
        for which, (left, right, scale, out) in enumerate((ups, downs)):
            grads = mxu(left[:, first : first + CHUNK], right, 0, 0)
            grads = grads[: rows.stop - first, :units]
            factor = columns[rows, 4 * which : 4 * which + 1]
            held[which, rows, :] = (grads * factor * scale).astype(bf16)
            copy = pltpu.make_async_copy(
                held.at[which, rows], out.at[rows], sems.at[len(copies)]
            )
            copy.start()
            copies.append(copy)
    for copy in copies:
        copy.wait()


def on_device(
    tokens,
    cotangent,
    codes_up,
    scales_up,
    codes_down,
    scales_down,
    up_rows,
    up_columns,
    down_rows,
    down_columns,
):
    width, units = codes_up.shape
    own = tokens.shape[0]
    wide = lax.axis_size("wide")
    narrow = lax.axis_size("narrow")
    chips = narrow // 2
    line = wide // 2
    count = own * narrow
    half = count // 2
    product = 2 * half * WIDTH * UNITS
    core_pairs = [(i, i ^ 1) for i in range(narrow)]
    same_core = [[2 * i + core for i in range(chips)] for core in range(2)]
    half_pairs = [(i, i ^ 1) for i in range(wide)]
    same_half = [[2 * i + part for i in range(line)] for part in range(2)]
    up_rows, down_rows = up_rows[None], down_rows[None]
    up_columns, down_columns = up_columns[None], down_columns[None]

    (copies,) = whole_call(spread_kernel, [((count, width), bf16)], "spread")(
        jnp.concatenate([tokens, cotangent], axis=0)
    )
    mine = lax.all_to_all(
        copies.reshape(chips, 2 * own, width),
        "narrow",
        0,
        0,
        axis_index_groups=same_core,
    ).reshape(count, width)
    w_up, w_down, digits = whole_call(
        weights_kernel,
        [((WIDTH, UNITS), bf16), ((WIDTH, UNITS), bf16), ((8, UNITS), f32)],
        "weights",
        scratch=[pltpu.VMEM((8, WIDTH), f32)],
    )(codes_up, scales_up.T, codes_down.T, scales_down, up_rows)
    mine, w_up, w_down, digits = lax.optimization_barrier((mine, w_up, w_down, digits))
    other = lax.ppermute(mine, "narrow", core_pairs)
    tok_own, cot_own, pre_own, slope_own = whole_call(
        functools.partial(first_kernel, own),
        [
            ((half, WIDTH), bf16),
            ((half, WIDTH), bf16),
            ((half, UNITS), bf16),
            ((half, UNITS), f32),
        ],
        "own_partial_sums",
        flops=3 * product,
    )(mine, w_up, w_down)
    tok, cot, parts = whole_call(
        functools.partial(partial_kernel, own, units),
        [((count, WIDTH), bf16), ((count, WIDTH), bf16), ((count, LANES), bf16)],
        "partial_sums",
        flops=5 * product,
    )(other, tok_own, cot_own, pre_own, slope_own, w_up, w_down, digits)

    parts = lax.all_to_all(
        parts.reshape(line, -1, LANES), "wide", 0, 0, axis_index_groups=same_half
    )
    sums = jnp.sum(parts.astype(f32), axis=0)
    sums = sums + lax.ppermute(sums.astype(bf16), "wide", half_pairs).astype(f32)
    pre = sums[:, :UNITS]
    acts = jnp.concatenate(
        [gelu_value(pre), sums[:, UNITS:SLOPE], sums[:, SLOPE:] * gelu_slope(pre)], axis=1
    ).astype(bf16)
    acts = lax.all_to_all(
        jnp.broadcast_to(acts[None], (line,) + acts.shape),
        "wide",
        0,
        0,
        axis_index_groups=same_half,
    ).reshape(count, LANES)

    send, stats, squares = whole_call(
        functools.partial(send_kernel, units),
        [((count + 16, WIDTH), bf16), ((8, STATS), f32), ((2, UNITS), f32)],
        "outputs_and_squares",
        flops=7 * product,
    )(acts, tok, cot, w_up, w_down, down_rows)
    got = lax.ppermute(send, "narrow", core_pairs)
    (keep,) = whole_call(
        functools.partial(keep_kernel, units),
        [((count, WIDTH), f32)],
        "own_outputs",
        flops=2 * product,
    )(acts, w_up, w_down)
    (mixed,) = whole_call(
        functools.partial(pair_kernel, own), [((count, WIDTH + STATS), bf16)], "pair_sum"
    )(keep, got, stats)
    mixed = lax.all_to_all(
        mixed.reshape(chips, -1, WIDTH + STATS), "narrow", 0, 0, axis_index_groups=same_core
    ).reshape(count, WIDTH + STATS)
    mlp_out, input_grad, step_up, step_down = whole_call(
        functools.partial(step_kernel, own, units),
        [
            ((own, width), bf16),
            ((own, width), bf16),
            ((width, units), bf16),
            ((width, units), bf16),
        ],
        "steps",
        scratch=[
            pltpu.VMEM((2, width, units), bf16),
            pltpu.SemaphoreType.DMA((2 * pl.cdiv(width, CHUNK),)),
        ],
        out_spaces=[pltpu.VMEM, pltpu.VMEM, pl.ANY, pl.ANY],
    )(mixed, acts, tok, cot, squares, up_rows, up_columns, down_rows, down_columns)
    return mlp_out, input_grad, step_up, step_down.T


def solution(mesh):
    return jax.shard_map(
        on_device,
        mesh=mesh,
        in_specs=(
            P("narrow", "wide"),
            P("narrow", "wide"),
            P("wide", "narrow"),
            P("wide", "narrow"),
            P("narrow", "wide"),
            P("narrow", "wide"),
            P("wide"),
            P("narrow"),
            P("narrow"),
            P("wide"),
        ),
        out_specs=(
            P("narrow", "wide"),
            P("narrow", "wide"),
            P("wide", "narrow"),
            P("narrow", "wide"),
        ),
        check_vma=False,
    )
```

```python
import functools

import jax
import jax.numpy as jnp
from jax import lax
from jax.experimental import pallas as pl
from jax.experimental.pallas import tpu as pltpu
from jax.sharding import PartitionSpec as P

D = 14848
FF = 30720
QB = 96

decay_rate = 0.9
square_eps = 1e-30

bf16 = jnp.bfloat16
f32 = jnp.float32

WIDTH = 1024
UNITS = 512
GRAM = 256
SLOPE = UNITS + GRAM
LANES = SLOPE + UNITS
DIGITS = 6
DIGIT_UNIT = 8.0
STATS = 256
SPARE = 160
CHUNK = 256


def gelu_value(value):
    return 0.5 * value * (1.0 + lax.erf(value * 0.7071067811865476))


def gelu_slope(value):
    return (
        0.5 * (1.0 + lax.erf(value * 0.7071067811865476))
        + value * jnp.exp(-0.5 * value * value) * 0.3989422804014327
    )


def mxu(left, right, left_dim=1, right_dim=0):
    return lax.dot_general(
        left, right, (((left_dim,), (right_dim,)), ((), ())), preferred_element_type=f32
    )


def iota(shape, dim):
    return lax.broadcasted_iota(jnp.int32, shape, dim)


def whole_call(kernel, outs, name, flops=0, scratch=(), out_spaces=None):
    spec = pl.BlockSpec(memory_space=pltpu.VMEM)
    spaces = out_spaces or [pltpu.VMEM] * len(outs)

    def call(*args):
        moved = sum(a.size * a.dtype.itemsize for a in args)
        return pl.pallas_call(
            kernel,
            out_shape=[jax.ShapeDtypeStruct(shape, dtype) for shape, dtype in outs],
            in_specs=[spec] * len(args),
            out_specs=[pl.BlockSpec(memory_space=space) for space in spaces],
            scratch_shapes=list(scratch),
            compiler_params=pltpu.CompilerParams(vmem_limit_bytes=24 * 1024 * 1024),
            cost_estimate=pl.CostEstimate(flops=flops, bytes_accessed=moved, transcendentals=0),
            name=name,
        )(*args)

    return call


def spread_kernel(packed, copies):
    both = packed[...].astype(f32)
    both = jnp.concatenate([both, both], axis=0).astype(bf16)
    for pair in range(copies.shape[0] // 16):
        copies[16 * pair : 16 * pair + 16, :] = both


def weights_kernel(codes_up, scales_up, codes_down, scales_down, up_rows, w_up, w_down, digits, lines):
    width, units = codes_up.shape
    lane = iota((width, units), 1)
    for codes, scales, ref in ((codes_up, scales_up, w_up), (codes_down, scales_down, w_down)):
        lines[...] = jnp.zeros_like(lines)
        lines[: units // QB, :width] = scales[...]
        columns = jnp.transpose(lines[...])[:width]
        spread = columns[:, 0:1]
        for group in range(1, units // QB):
            spread = jnp.where(lane >= group * QB, columns[:, group : group + 1], spread)
        ref[...] = jnp.zeros_like(ref)
        ref[:width, :units] = (codes[...].astype(f32) * spread).astype(bf16)
    place = iota((8, UNITS), 1)
    line = jnp.zeros((8, UNITS), f32)
    rest = jnp.floor(jnp.sum(up_rows[...], axis=1, keepdims=True) * DIGIT_UNIT + 0.5)
    for digit in range(DIGITS):
        shorter = jnp.floor(rest * (1.0 / 16.0))
        line = jnp.where(place == units + 1 + digit, rest - 16.0 * shorter, line)
        rest = shorter
    digits[...] = line


def apart(count, own):
    half = count // 2
    row, column = iota((count, count), 0), iota((count, count), 1)
    second = (row >= half).astype(jnp.int32)
    token = row - second * half
    source = (token // own) * (2 * own) + second * own + token % own
    return (column == source).astype(f32).astype(bf16)


def first_kernel(own, mine, w_up, w_down, tok, cot, pre, slope):
    count, width = mine.shape
    half = count // 2
    rows = mxu(apart(count, own), mine[...]).astype(bf16)
    for ref, first in ((tok, 0), (cot, half)):
        ref[:, WIDTH - 128 :] = jnp.zeros((half, 128), bf16)
        ref[:, :width] = rows[first : first + half]
    pre[...] = mxu(tok[...], w_up[...]).astype(bf16)
    slope[...] = mxu(cot[...], w_down[...])


def partial_kernel(
    own, units, other, tok_own, cot_own, pre_own, slope_own, w_up, w_down, digits, tok, cot, parts
):
    count, width = other.shape
    half = count // 2
    rows = mxu(apart(count, own), other[...]).astype(bf16)
    for ref, first, owned in ((tok, 0, tok_own), (cot, half, cot_own)):
        ref[:half, :] = owned[...]
        ref[half:, WIDTH - 128 :] = jnp.zeros((half, 128), bf16)
        ref[half:, :width] = rows[first : first + half]
    parts[:half, :UNITS] = pre_own[...]
    parts[half:, :UNITS] = mxu(tok[half:, :], w_up[...]).astype(bf16)
    row, column = iota((count, count), 0), iota((count, count), 1)
    tokens, cotangents = tok[...], cot[...]
    gram_tok = mxu(tokens, tokens, 1, 1)
    gram_cot = mxu(cotangents, cotangents, 1, 1)
    parts[:, UNITS:SLOPE] = jnp.where(row >= column, gram_tok, gram_cot).astype(bf16)
    diagonal = jnp.sum(jnp.where(row == column, gram_cot, 0.0), axis=1, keepdims=True)
    lane = iota((half, UNITS), 1)
    extra = digits[0:1, :]
    slope = jnp.where(lane == units, diagonal[:half], slope_own[...] + extra)
    parts[:half, SLOPE:] = slope.astype(bf16)
    slope = mxu(cot[half:, :], w_down[...])
    slope = jnp.where(lane == units, diagonal[half:], slope + extra)
    parts[half:, SLOPE:] = slope.astype(bf16)


def masked_slope(acts, units):
    count = acts.shape[0]
    lane = iota((count, UNITS), 1)
    return jnp.where(lane < units, acts[:, SLOPE:].astype(f32), 0.0)


def send_kernel(units, acts, tok, cot, w_up, w_down, down_rows, send, stats, squares):
    count = acts.shape[0]
    half = count // 2
    hidden = acts[:, :UNITS]
    d_wide = masked_slope(acts, units)
    diagonal = 2.0 * acts[:, SLOPE:].astype(f32)[:, units : units + 1]
    d_pre = d_wide.astype(bf16)
    send[:half, :] = mxu(hidden[half:], w_down[...], 1, 1).astype(bf16)
    send[half:count, :] = mxu(d_pre[half:], w_up[...], 1, 1).astype(bf16)
    row, column = iota((count, count), 0), iota((count, count), 1)
    gram = acts[:, UNITS:SLOPE].astype(f32)
    lower = jnp.where(row > column, 2.0 * gram, jnp.where(row == column, gram, 0.0)).astype(bf16)
    upper = jnp.where(row < column, 2.0 * gram, 0.0).astype(bf16)
    hidden_wide = hidden.astype(f32)
    colsq_up = jnp.sum(d_wide * mxu(lower, d_pre), axis=0, keepdims=True)
    rowsq_down = jnp.sum(
        hidden_wide * (mxu(upper, hidden) + diagonal * hidden_wide), axis=0, keepdims=True
    )
    real = iota((1, UNITS), 1) < units
    colsq_up = jnp.where(real, jnp.maximum(colsq_up, 0.0) + D * square_eps, 0.0)
    rowsq_down = jnp.where(real, jnp.maximum(rowsq_down, 0.0) + D * square_eps, 0.0)
    squares[0:1, :] = colsq_up
    squares[1:2, :] = rowsq_down
    totals = [
        jnp.sum(colsq_up, axis=1, keepdims=True),
        jnp.sum(rowsq_down, axis=1, keepdims=True),
        jnp.sum(down_rows[...], axis=1, keepdims=True),
    ]
    g_up = mxu(d_pre, tok[...], 0, 0)
    rowsq_up = jnp.sum(g_up * g_up, axis=0, keepdims=True) + units * square_eps
    g_down = mxu(hidden, cot[...], 0, 0)
    colsq_down = jnp.sum(g_down * g_down, axis=0, keepdims=True) + units * square_eps
    spare = iota((1, STATS), 1)
    for place, sums in ((0, rowsq_up), (4, colsq_down)):
        for part in range(4):
            piece = sums[:, part * STATS : (part + 1) * STATS]
            if part == 3:
                piece = jnp.where(spare < SPARE, piece, 0.0)
                for index, total in enumerate(totals):
                    piece = jnp.where(spare == SPARE + index, total, piece)
            stats[place + part : place + part + 1, :] = piece
    block = stats[...]
    high = block.astype(bf16).astype(f32)
    send[count:, :] = jnp.zeros((16, WIDTH), bf16)
    send[count:, :STATS] = jnp.concatenate([high, block - high], axis=0).astype(bf16)


def keep_kernel(units, acts, w_up, w_down, keep):
    half = acts.shape[0] // 2
    keep[:half, :] = mxu(acts[:half, :UNITS], w_down[...], 1, 1)
    d_pre = masked_slope(acts, units)[:half].astype(bf16)
    keep[half:, :] = mxu(d_pre, w_up[...], 1, 1)


def pair_kernel(own, keep, got, stats, mixed):
    count = keep.shape[0]
    sums = (keep[...] + got[:count, :].astype(f32)).astype(bf16)
    mixed[:, :WIDTH] = mxu(apart(count, own), sums, 0, 0).astype(bf16)
    tail = got[count:, :STATS].astype(f32)
    block = stats[...] + (tail[:8] + tail[8:])
    high = block.astype(bf16).astype(f32)
    low = (iota((8, STATS), 0) == 7) & (iota((8, STATS), 1) >= SPARE)
    block = jnp.where(low, block - high, high)
    mixed[:, WIDTH:] = jnp.concatenate([block] * (count // 8), axis=0).astype(bf16)


def padded(line, lanes):
    return jnp.concatenate([line, jnp.ones((1, lanes - line.shape[1]), f32)], axis=1)


def step_kernel(
    own,
    units,
    mixed,
    acts,
    tok,
    cot,
    squares,
    up_rows,
    up_columns,
    down_rows,
    down_columns,
    mlp_out,
    input_grad,
    step_up,
    step_down,
    held,
    factors,
    sems,
):
    width = up_rows.shape[1]
    sums = jnp.sum(mixed[...].astype(f32).reshape(-1, 2 * own, WIDTH + STATS), axis=0)
    mlp_out[...] = sums[:own, :width].astype(bf16)
    input_grad[...] = sums[own:, :width].astype(bf16)
    block = sums[:, WIDTH:]
    rowsq_up = jnp.concatenate([block[i : i + 1] for i in range(4)], axis=1)
    colsq_down = jnp.concatenate([block[i : i + 1] for i in range(4, 8)], axis=1)
    both = block[3:4] + block[7:8]
    spare = iota((1, STATS), 1)
    total_up, total_down, total_rows = (
        jnp.sum(jnp.where(spare == SPARE + i, both, 0.0), axis=1, keepdims=True) for i in range(3)
    )
    digits = acts[0:16, SLOPE:].astype(f32)[0:1]
    lane = iota((1, UNITS), 1)
    weight = jnp.zeros((1, UNITS), f32)
    for digit in range(DIGITS):
        weight = jnp.where(lane == units + 1 + digit, 2.0 * 16.0**digit / DIGIT_UNIT, weight)
    total_state = jnp.sum(digits * weight, axis=1, keepdims=True)
    mean_up = (decay_rate * total_state + (1.0 - decay_rate) * total_up / FF) / D
    mean_down = (decay_rate * total_rows + (1.0 - decay_rate) * total_down / D) / FF
    keep_rate = 1.0 - decay_rate
    row_new_up = decay_rate * up_rows[...] + keep_rate * rowsq_up[:, :width] / FF
    col_new_down = decay_rate * down_columns[...] + keep_rate * colsq_down[:, :width] / FF
    lines = jnp.concatenate(
        [
            jnp.broadcast_to(padded(lax.rsqrt(row_new_up) * jnp.sqrt(mean_up), WIDTH), (4, WIDTH)),
            jnp.broadcast_to(
                padded(lax.rsqrt(col_new_down) * jnp.sqrt(mean_down), WIDTH), (4, WIDTH)
            ),
        ],
        axis=0,
    )
    high = lines.astype(bf16)
    rest = lines - high.astype(f32)
    middle = rest.astype(bf16)
    low = (rest - middle.astype(f32)).astype(bf16)
    pieces = [jnp.concatenate([p[4 * i : 4 * i + 4] for p in (high, middle, low)], axis=0) for i in (0, 1)]
    for which in (0, 1):
        one = (iota((16, WIDTH), 0) % 4 == 0) & (iota((16, WIDTH), 0) < 12)
        part = jnp.concatenate([pieces[which].astype(f32), jnp.zeros((4, WIDTH), f32)], axis=0)
        factors[which] = jnp.where(one, part, 0.0).astype(bf16)
    col_new_up = decay_rate * up_columns[...] + keep_rate * squares[0:1, :units] / D
    row_new_down = decay_rate * down_rows[...] + keep_rate * squares[1:2, :units] / D
    ups = (tok, acts[:, SLOPE:], padded(lax.rsqrt(col_new_up), UNITS), step_up)
    downs = (cot, acts[:, :UNITS], padded(lax.rsqrt(row_new_down), UNITS), step_down)
    ones = jnp.ones((16, UNITS), bf16)

    def copy_of(which, first, length, index, out):
        return pltpu.make_async_copy(
            held.at[which, pl.ds(first, length)], out.at[pl.ds(first, length)], sems.at[index]
        )

    def chunk(first, length, index):
        lanes = pl.ds(first, CHUNK)
        for which, (left, right, scale, out) in enumerate((ups, downs)):
            factor = mxu(factors[which, :, lanes], ones, 0, 0)
            grads = mxu(left[:, lanes], right, 0, 0) * factor * scale
            held[which, pl.ds(first, length), :] = grads[:length, :units].astype(bf16)
            copy_of(which, first, length, 2 * index + which, out).start()

    whole = width // CHUNK

    for index in range(whole):
        chunk(index * CHUNK, CHUNK, index)

    if width % CHUNK:
        chunk(whole * CHUNK, width % CHUNK, whole)
    for index in range(pl.cdiv(width, CHUNK)):
        first = index * CHUNK
        for which, out in enumerate((step_up, step_down)):
            copy_of(which, first, min(CHUNK, width - first), 2 * index + which, out).wait()


def on_device(
    tokens,
    cotangent,
    codes_up,
    scales_up,
    codes_down,
    scales_down,
    up_rows,
    up_columns,
    down_rows,
    down_columns,
):
    width, units = codes_up.shape
    own = tokens.shape[0]
    wide = lax.axis_size("wide")
    narrow = lax.axis_size("narrow")
    chips = narrow // 2
    line = wide // 2
    count = own * narrow
    half = count // 2
    product = 2 * half * WIDTH * UNITS
    core_pairs = [(i, i ^ 1) for i in range(narrow)]
    same_core = [[2 * i + core for i in range(chips)] for core in range(2)]
    half_pairs = [(i, i ^ 1) for i in range(wide)]
    same_half = [[2 * i + part for i in range(line)] for part in range(2)]
    up_rows, down_rows = up_rows[None], down_rows[None]
    up_columns, down_columns = up_columns[None], down_columns[None]

    (copies,) = whole_call(spread_kernel, [((count, width), bf16)], "spread")(
        jnp.concatenate([tokens, cotangent], axis=0)
    )
    mine = lax.all_to_all(
        copies.reshape(chips, 2 * own, width),
        "narrow",
        0,
        0,
        axis_index_groups=same_core,
    ).reshape(count, width)
    w_up, w_down, digits = whole_call(
        weights_kernel,
        [((WIDTH, UNITS), bf16), ((WIDTH, UNITS), bf16), ((8, UNITS), f32)],
        "weights",
        scratch=[pltpu.VMEM((8, WIDTH), f32)],
    )(codes_up, scales_up.T, codes_down.T, scales_down, up_rows)
    mine, w_up, w_down, digits = lax.optimization_barrier((mine, w_up, w_down, digits))
    other = lax.ppermute(mine, "narrow", core_pairs)
    tok_own, cot_own, pre_own, slope_own = whole_call(
        functools.partial(first_kernel, own),
        [
            ((half, WIDTH), bf16),
            ((half, WIDTH), bf16),
            ((half, UNITS), bf16),
            ((half, UNITS), f32),
        ],
        "own_partial_sums",
        flops=3 * product,
    )(mine, w_up, w_down)
    tok, cot, parts = whole_call(
        functools.partial(partial_kernel, own, units),
        [((count, WIDTH), bf16), ((count, WIDTH), bf16), ((count, LANES), bf16)],
        "partial_sums",
        flops=5 * product,
    )(other, tok_own, cot_own, pre_own, slope_own, w_up, w_down, digits)

    parts = lax.all_to_all(
        parts.reshape(line, -1, LANES), "wide", 0, 0, axis_index_groups=same_half
    )
    sums = jnp.sum(parts.astype(f32), axis=0)
    sums = sums + lax.ppermute(sums.astype(bf16), "wide", half_pairs).astype(f32)
    pre = sums[:, :UNITS]
    acts = jnp.concatenate(
        [gelu_value(pre), sums[:, UNITS:SLOPE], sums[:, SLOPE:] * gelu_slope(pre)], axis=1
    ).astype(bf16)
    acts = lax.all_to_all(
        jnp.broadcast_to(acts[None], (line,) + acts.shape),
        "wide",
        0,
        0,
        axis_index_groups=same_half,
    ).reshape(count, LANES)

    send, stats, squares = whole_call(
        functools.partial(send_kernel, units),
        [((count + 16, WIDTH), bf16), ((8, STATS), f32), ((2, UNITS), f32)],
        "outputs_and_squares",
        flops=7 * product,
    )(acts, tok, cot, w_up, w_down, down_rows)
    got = lax.ppermute(send, "narrow", core_pairs)
    (keep,) = whole_call(
        functools.partial(keep_kernel, units),
        [((count, WIDTH), f32)],
        "own_outputs",
        flops=2 * product,
    )(acts, w_up, w_down)
    (mixed,) = whole_call(
        functools.partial(pair_kernel, own), [((count, WIDTH + STATS), bf16)], "pair_sum"
    )(keep, got, stats)
    mixed = lax.all_to_all(
        mixed.reshape(chips, -1, WIDTH + STATS), "narrow", 0, 0, axis_index_groups=same_core
    ).reshape(count, WIDTH + STATS)
    mlp_out, input_grad, step_up, step_down = whole_call(
        functools.partial(step_kernel, own, units),
        [
            ((own, width), bf16),
            ((own, width), bf16),
            ((width, units), bf16),
            ((width, units), bf16),
        ],
        "steps",
        scratch=[
            pltpu.VMEM((2, width, units), bf16),
            pltpu.VMEM((2, 16, WIDTH), bf16),
            pltpu.SemaphoreType.DMA((2 * pl.cdiv(width, CHUNK),)),
        ],
        out_spaces=[pltpu.VMEM, pltpu.VMEM, pl.ANY, pl.ANY],
    )(mixed, acts, tok, cot, squares, up_rows, up_columns, down_rows, down_columns)
    return mlp_out, input_grad, step_up, step_down.T


def solution(mesh):
    return jax.shard_map(
        on_device,
        mesh=mesh,
        in_specs=(
            P("narrow", "wide"),
            P("narrow", "wide"),
            P("wide", "narrow"),
            P("wide", "narrow"),
            P("narrow", "wide"),
            P("narrow", "wide"),
            P("wide"),
            P("narrow"),
            P("narrow"),
            P("wide"),
        ),
        out_specs=(
            P("narrow", "wide"),
            P("narrow", "wide"),
            P("wide", "narrow"),
            P("narrow", "wide"),
        ),
        check_vma=False,
    )
```

```python
import functools

import jax
import jax.numpy as jnp
from jax import lax
from jax.experimental import pallas as pl
from jax.experimental.pallas import tpu as pltpu
from jax.sharding import PartitionSpec as P

D = 14848
FF = 30720
QB = 96

decay_rate = 0.9
square_eps = 1e-30

bf16 = jnp.bfloat16
f32 = jnp.float32

WIDTH = 1024
UNITS = 512
GRAM = 256
SLOPE = UNITS + GRAM
LANES = SLOPE + UNITS
DIGITS = 6
DIGIT_UNIT = 8.0
STATS = 256
SPARE = 160
CHUNK = 256


def gelu_value(value):
    return 0.5 * value * (1.0 + lax.erf(value * 0.7071067811865476))


def gelu_slope(value):
    return (
        0.5 * (1.0 + lax.erf(value * 0.7071067811865476))
        + value * jnp.exp(-0.5 * value * value) * 0.3989422804014327
    )


def mxu(left, right, left_dim=1, right_dim=0):
    return lax.dot_general(
        left, right, (((left_dim,), (right_dim,)), ((), ())), preferred_element_type=f32
    )


def iota(shape, dim):
    return lax.broadcasted_iota(jnp.int32, shape, dim)


def whole_call(kernel, outs, name, flops=0, scratch=(), out_spaces=None):
    spec = pl.BlockSpec(memory_space=pltpu.VMEM)
    spaces = out_spaces or [pltpu.VMEM] * len(outs)

    def call(*args):
        moved = sum(a.size * a.dtype.itemsize for a in args)
        return pl.pallas_call(
            kernel,
            out_shape=[jax.ShapeDtypeStruct(shape, dtype) for shape, dtype in outs],
            in_specs=[spec] * len(args),
            out_specs=[pl.BlockSpec(memory_space=space) for space in spaces],
            scratch_shapes=list(scratch),
            compiler_params=pltpu.CompilerParams(vmem_limit_bytes=10 * 1024 * 1024),
            cost_estimate=pl.CostEstimate(flops=flops, bytes_accessed=moved, transcendentals=0),
            name=name,
        )(*args)

    return call


def spread_kernel(packed, copies):
    both = packed[...].astype(f32)
    both = jnp.concatenate([both, both], axis=0).astype(bf16)
    for pair in range(copies.shape[0] // 16):
        copies[16 * pair : 16 * pair + 16, :] = both


def weights_kernel(codes_up, scales_up, codes_down, scales_down, up_rows, w_up, w_down, digits, lines):
    width, units = codes_up.shape
    lane = iota((width, units), 1)
    for codes, scales, ref in ((codes_up, scales_up, w_up), (codes_down, scales_down, w_down)):
        lines[...] = jnp.zeros_like(lines)
        lines[: units // QB, :width] = scales[...]
        columns = jnp.transpose(lines[...])[:width]
        spread = columns[:, 0:1]
        for group in range(1, units // QB):
            spread = jnp.where(lane >= group * QB, columns[:, group : group + 1], spread)
        ref[...] = jnp.zeros_like(ref)
        ref[:width, :units] = (codes[...].astype(f32) * spread).astype(bf16)
    place = iota((8, UNITS), 1)
    line = jnp.zeros((8, UNITS), f32)
    rest = jnp.floor(jnp.sum(up_rows[...], axis=1, keepdims=True) * DIGIT_UNIT + 0.5)
    for digit in range(DIGITS):
        shorter = jnp.floor(rest * (1.0 / 16.0))
        line = jnp.where(place == units + 1 + digit, rest - 16.0 * shorter, line)
        rest = shorter
    digits[...] = line


def apart(count, own):
    half = count // 2
    row, column = iota((count, count), 0), iota((count, count), 1)
    second = (row >= half).astype(jnp.int32)
    token = row - second * half
    source = (token // own) * (2 * own) + second * own + token % own
    return (column == source).astype(f32).astype(bf16)


def first_kernel(own, mine, w_up, w_down, tok, cot, pre, slope):
    count, width = mine.shape
    half = count // 2
    rows = mxu(apart(count, own), mine[...]).astype(bf16)
    for ref, first in ((tok, 0), (cot, half)):
        ref[:, WIDTH - 128 :] = jnp.zeros((half, 128), bf16)
        ref[:, :width] = rows[first : first + half]
    pre[...] = mxu(tok[...], w_up[...]).astype(bf16)
    slope[...] = mxu(cot[...], w_down[...])


def partial_kernel(
    own, units, other, tok_own, cot_own, pre_own, slope_own, w_up, w_down, digits, tok, cot, parts
):
    count, width = other.shape
    half = count // 2
    rows = mxu(apart(count, own), other[...]).astype(bf16)
    for ref, first, owned in ((tok, 0, tok_own), (cot, half, cot_own)):
        ref[:half, :] = owned[...]
        ref[half:, WIDTH - 128 :] = jnp.zeros((half, 128), bf16)
        ref[half:, :width] = rows[first : first + half]
    parts[:half, :UNITS] = pre_own[...]
    parts[half:, :UNITS] = mxu(tok[half:, :], w_up[...]).astype(bf16)
    row, column = iota((count, count), 0), iota((count, count), 1)
    tokens, cotangents = tok[...], cot[...]
    gram_tok = mxu(tokens, tokens, 1, 1)
    gram_cot = mxu(cotangents, cotangents, 1, 1)
    parts[:, UNITS:SLOPE] = jnp.where(row >= column, gram_tok, gram_cot).astype(bf16)
    diagonal = jnp.sum(jnp.where(row == column, gram_cot, 0.0), axis=1, keepdims=True)
    lane = iota((half, UNITS), 1)
    extra = digits[0:1, :]
    slope = jnp.where(lane == units, diagonal[:half], slope_own[...] + extra)
    parts[:half, SLOPE:] = slope.astype(bf16)
    slope = mxu(cot[half:, :], w_down[...])
    slope = jnp.where(lane == units, diagonal[half:], slope + extra)
    parts[half:, SLOPE:] = slope.astype(bf16)


def masked_slope(acts, units):
    count = acts.shape[0]
    lane = iota((count, UNITS), 1)
    return jnp.where(lane < units, acts[:, SLOPE:].astype(f32), 0.0)


def send_kernel(units, acts, tok, cot, w_up, w_down, down_rows, send, stats, squares):
    count = acts.shape[0]
    half = count // 2
    hidden = acts[:, :UNITS]
    d_wide = masked_slope(acts, units)
    diagonal = 2.0 * acts[:, SLOPE:].astype(f32)[:, units : units + 1]
    d_pre = d_wide.astype(bf16)
    send[:half, :] = mxu(hidden[half:], w_down[...], 1, 1).astype(bf16)
    send[half:count, :] = mxu(d_pre[half:], w_up[...], 1, 1).astype(bf16)
    row, column = iota((count, count), 0), iota((count, count), 1)
    gram = acts[:, UNITS:SLOPE].astype(f32)
    lower = jnp.where(row > column, 2.0 * gram, jnp.where(row == column, gram, 0.0)).astype(bf16)
    upper = jnp.where(row < column, 2.0 * gram, 0.0).astype(bf16)
    hidden_wide = hidden.astype(f32)
    colsq_up = jnp.sum(d_wide * mxu(lower, d_pre), axis=0, keepdims=True)
    rowsq_down = jnp.sum(
        hidden_wide * (mxu(upper, hidden) + diagonal * hidden_wide), axis=0, keepdims=True
    )
    real = iota((1, UNITS), 1) < units
    colsq_up = jnp.where(real, jnp.maximum(colsq_up, 0.0) + D * square_eps, 0.0)
    rowsq_down = jnp.where(real, jnp.maximum(rowsq_down, 0.0) + D * square_eps, 0.0)
    squares[0:1, :] = colsq_up
    squares[1:2, :] = rowsq_down
    totals = [
        jnp.sum(colsq_up, axis=1, keepdims=True),
        jnp.sum(rowsq_down, axis=1, keepdims=True),
        jnp.sum(down_rows[...], axis=1, keepdims=True),
    ]
    g_up = mxu(d_pre, tok[...], 0, 0)
    rowsq_up = jnp.sum(g_up * g_up, axis=0, keepdims=True) + units * square_eps
    g_down = mxu(hidden, cot[...], 0, 0)
    colsq_down = jnp.sum(g_down * g_down, axis=0, keepdims=True) + units * square_eps
    spare = iota((1, STATS), 1)
    for place, sums in ((0, rowsq_up), (4, colsq_down)):
        for part in range(4):
            piece = sums[:, part * STATS : (part + 1) * STATS]
            if part == 3:
                piece = jnp.where(spare < SPARE, piece, 0.0)
                for index, total in enumerate(totals):
                    piece = jnp.where(spare == SPARE + index, total, piece)
            stats[place + part : place + part + 1, :] = piece
    block = stats[...]
    high = block.astype(bf16).astype(f32)
    send[count:, :] = jnp.zeros((16, WIDTH), bf16)
    send[count:, :STATS] = jnp.concatenate([high, block - high], axis=0).astype(bf16)


def keep_kernel(units, acts, w_up, w_down, keep):
    half = acts.shape[0] // 2
    keep[:half, :] = mxu(acts[:half, :UNITS], w_down[...], 1, 1)
    d_pre = masked_slope(acts, units)[:half].astype(bf16)
    keep[half:, :] = mxu(d_pre, w_up[...], 1, 1)


def pair_kernel(own, keep, got, stats, mixed):
    count = keep.shape[0]
    sums = (keep[...] + got[:count, :].astype(f32)).astype(bf16)
    mixed[:, :WIDTH] = mxu(apart(count, own), sums, 0, 0).astype(bf16)
    tail = got[count:, :STATS].astype(f32)
    block = stats[...] + (tail[:8] + tail[8:])
    high = block.astype(bf16).astype(f32)
    low = (iota((8, STATS), 0) == 7) & (iota((8, STATS), 1) >= SPARE)
    block = jnp.where(low, block - high, high)
    mixed[:, WIDTH:] = jnp.concatenate([block] * (count // 8), axis=0).astype(bf16)


def padded(line, lanes):
    return jnp.concatenate([line, jnp.ones((1, lanes - line.shape[1]), f32)], axis=1)


def step_kernel(
    own,
    units,
    mixed,
    acts,
    tok,
    cot,
    squares,
    up_rows,
    up_columns,
    down_rows,
    down_columns,
    mlp_out,
    input_grad,
    step_up,
    step_down,
    held,
    sems,
):
    width = up_rows.shape[1]
    sums = jnp.sum(mixed[...].astype(f32).reshape(-1, 2 * own, WIDTH + STATS), axis=0)
    mlp_out[...] = sums[:own, :width].astype(bf16)
    input_grad[...] = sums[own:, :width].astype(bf16)
    block = sums[:, WIDTH:]
    rowsq_up = jnp.concatenate([block[i : i + 1] for i in range(4)], axis=1)
    colsq_down = jnp.concatenate([block[i : i + 1] for i in range(4, 8)], axis=1)
    both = block[3:4] + block[7:8]
    spare = iota((1, STATS), 1)
    total_up, total_down, total_rows = (
        jnp.sum(jnp.where(spare == SPARE + i, both, 0.0), axis=1, keepdims=True) for i in range(3)
    )
    digits = acts[0:16, SLOPE:].astype(f32)[0:1]
    lane = iota((1, UNITS), 1)
    weight = jnp.zeros((1, UNITS), f32)
    for digit in range(DIGITS):
        weight = jnp.where(lane == units + 1 + digit, 2.0 * 16.0**digit / DIGIT_UNIT, weight)
    total_state = jnp.sum(digits * weight, axis=1, keepdims=True)
    mean_up = (decay_rate * total_state + (1.0 - decay_rate) * total_up / FF) / D
    mean_down = (decay_rate * total_rows + (1.0 - decay_rate) * total_down / D) / FF
    keep_rate = 1.0 - decay_rate
    row_new_up = decay_rate * up_rows[...] + keep_rate * rowsq_up[:, :width] / FF
    col_new_down = decay_rate * down_columns[...] + keep_rate * colsq_down[:, :width] / FF
    lines = jnp.concatenate(
        [
            jnp.broadcast_to(padded(lax.rsqrt(row_new_up) * jnp.sqrt(mean_up), WIDTH), (4, WIDTH)),
            jnp.broadcast_to(
                padded(lax.rsqrt(col_new_down) * jnp.sqrt(mean_down), WIDTH), (4, WIDTH)
            ),
        ],
        axis=0,
    )
    columns = jnp.transpose(lines)
    col_new_up = decay_rate * up_columns[...] + keep_rate * squares[0:1, :units] / D
    row_new_down = decay_rate * down_rows[...] + keep_rate * squares[1:2, :units] / D
    ups = (tok, acts[:, SLOPE:], lax.rsqrt(col_new_up), step_up)
    downs = (cot, acts[:, :UNITS], lax.rsqrt(row_new_down), step_down)
    copies = []
    for first in range(0, width, CHUNK):
        rows = slice(first, min(first + CHUNK, width))
        for which, (left, right, scale, out) in enumerate((ups, downs)):
            grads = mxu(left[:, first : first + CHUNK], right, 0, 0)
            grads = grads[: rows.stop - first, :units]
            factor = columns[rows, 4 * which : 4 * which + 1]
            held[which, rows, :] = (grads * factor * scale).astype(bf16)
            copy = pltpu.make_async_copy(
                held.at[which, rows], out.at[rows], sems.at[len(copies)]
            )
            copy.start()
            copies.append(copy)
    for copy in copies:
        copy.wait()


def on_device(
    tokens,
    cotangent,
    codes_up,
    scales_up,
    codes_down,
    scales_down,
    up_rows,
    up_columns,
    down_rows,
    down_columns,
):
    width, units = codes_up.shape
    own = tokens.shape[0]
    wide = lax.axis_size("wide")
    narrow = lax.axis_size("narrow")
    chips = narrow // 2
    line = wide // 2
    count = own * narrow
    half = count // 2
    product = 2 * half * WIDTH * UNITS
    core_pairs = [(i, i ^ 1) for i in range(narrow)]
    same_core = [[2 * i + core for i in range(chips)] for core in range(2)]
    half_pairs = [(i, i ^ 1) for i in range(wide)]
    same_half = [[2 * i + part for i in range(line)] for part in range(2)]
    up_rows, down_rows = up_rows[None], down_rows[None]
    up_columns, down_columns = up_columns[None], down_columns[None]

    (copies,) = whole_call(spread_kernel, [((count, width), bf16)], "spread")(
        jnp.concatenate([tokens, cotangent], axis=0)
    )
    mine = lax.all_to_all(
        copies.reshape(chips, 2 * own, width),
        "narrow",
        0,
        0,
        axis_index_groups=same_core,
    ).reshape(count, width)
    w_up, w_down, digits = whole_call(
        weights_kernel,
        [((WIDTH, UNITS), bf16), ((WIDTH, UNITS), bf16), ((8, UNITS), f32)],
        "weights",
        scratch=[pltpu.VMEM((8, WIDTH), f32)],
    )(codes_up, scales_up.T, codes_down.T, scales_down, up_rows)
    mine, w_up, w_down, digits = lax.optimization_barrier((mine, w_up, w_down, digits))
    other = lax.ppermute(mine, "narrow", core_pairs)
    tok_own, cot_own, pre_own, slope_own = whole_call(
        functools.partial(first_kernel, own),
        [
            ((half, WIDTH), bf16),
            ((half, WIDTH), bf16),
            ((half, UNITS), bf16),
            ((half, UNITS), f32),
        ],
        "own_partial_sums",
        flops=3 * product,
    )(mine, w_up, w_down)
    tok, cot, parts = whole_call(
        functools.partial(partial_kernel, own, units),
        [((count, WIDTH), bf16), ((count, WIDTH), bf16), ((count, LANES), bf16)],
        "partial_sums",
        flops=5 * product,
    )(other, tok_own, cot_own, pre_own, slope_own, w_up, w_down, digits)

    parts = lax.all_to_all(
        parts.reshape(line, -1, LANES), "wide", 0, 0, axis_index_groups=same_half
    )
    sums = jnp.sum(parts.astype(f32), axis=0)
    sums = sums + lax.ppermute(sums.astype(bf16), "wide", half_pairs).astype(f32)
    pre = sums[:, :UNITS]
    acts = jnp.concatenate(
        [gelu_value(pre), sums[:, UNITS:SLOPE], sums[:, SLOPE:] * gelu_slope(pre)], axis=1
    ).astype(bf16)
    acts = lax.all_to_all(
        jnp.broadcast_to(acts[None], (line,) + acts.shape),
        "wide",
        0,
        0,
        axis_index_groups=same_half,
    ).reshape(count, LANES)

    send, stats, squares = whole_call(
        functools.partial(send_kernel, units),
        [((count + 16, WIDTH), bf16), ((8, STATS), f32), ((2, UNITS), f32)],
        "outputs_and_squares",
        flops=7 * product,
    )(acts, tok, cot, w_up, w_down, down_rows)
    got = lax.ppermute(send, "narrow", core_pairs)
    (keep,) = whole_call(
        functools.partial(keep_kernel, units),
        [((count, WIDTH), f32)],
        "own_outputs",
        flops=2 * product,
    )(acts, w_up, w_down)
    (mixed,) = whole_call(
        functools.partial(pair_kernel, own), [((count, WIDTH + STATS), bf16)], "pair_sum"
    )(keep, got, stats)
    mixed = lax.all_to_all(
        mixed.reshape(chips, -1, WIDTH + STATS), "narrow", 0, 0, axis_index_groups=same_core
    ).reshape(count, WIDTH + STATS)
    mlp_out, input_grad, step_up, step_down = whole_call(
        functools.partial(step_kernel, own, units),
        [
            ((own, width), bf16),
            ((own, width), bf16),
            ((width, units), bf16),
            ((width, units), bf16),
        ],
        "steps",
        scratch=[
            pltpu.VMEM((2, width, units), bf16),
            pltpu.SemaphoreType.DMA((2 * pl.cdiv(width, CHUNK),)),
        ],
        out_spaces=[pltpu.VMEM, pltpu.VMEM, pl.ANY, pl.ANY],
    )(mixed, acts, tok, cot, squares, up_rows, up_columns, down_rows, down_columns)
    return mlp_out, input_grad, step_up, step_down.T


def solution(mesh):
    return jax.shard_map(
        on_device,
        mesh=mesh,
        in_specs=(
            P("narrow", "wide"),
            P("narrow", "wide"),
            P("wide", "narrow"),
            P("wide", "narrow"),
            P("narrow", "wide"),
            P("narrow", "wide"),
            P("wide"),
            P("narrow"),
            P("narrow"),
            P("wide"),
        ),
        out_specs=(
            P("narrow", "wide"),
            P("narrow", "wide"),
            P("wide", "narrow"),
            P("narrow", "wide"),
        ),
        check_vma=False,
    )
```
